32 devices in a mesh: groups: 2 (over y), expert: 16 (over z, x, core), dp: 1.
Axes of the slice: x: 2, y: 2, z: 4, core: 2. Of those that a mesh axis runs over, the one named last changes fastest.
Arguments:
- tokens: bfloat16 [128, 3584], P(('groups', 'expert', 'dp')), parts along dimension 0, may hold values from -6 to 6
- cotangent: bfloat16 [128, 3584], P(('groups', 'expert', 'dp')), parts along dimension 0, may hold values from -6 to 6
- gate: bfloat16 [128, 8], P(('groups', 'expert', 'dp')), parts along dimension 0, may hold values from 0.019897461 to 0.5
- expert_ids: int32 [128, 8], P(('groups', 'expert', 'dp')), parts along dimension 0, may hold values from 0 to 15, all different within a row; in each aligned block of 4 rows (0 to 3, 4 to 7, ...) at most 4 rows name the same one
- w_in: bfloat16 [16, 3584, 1024], P('expert', None, 'dp'), may hold values from -0.09375 to 0.09375
- w_out: bfloat16 [16, 1024, 3584], P('expert', 'dp'), may hold values from -0.1875 to 0.1875
Outputs:
- tokens_grad: bfloat16 [128, 3584], P(('groups', 'expert', 'dp')), parts along dimension 0
- gate_grad: float32 [128, 8], P(('groups', 'expert', 'dp')), parts along dimension 0
- w_in_grad: bfloat16 [32, 3584, 1024], P(('groups', 'expert'), None, 'dp'), parts along dimension 0
- w_out_grad: bfloat16 [32, 1024, 3584], P(('groups', 'expert'), 'dp'), parts along dimension 0
The draws below stay inside these ranges and needn't reach their ends.
There are 2 independent parts, one for each index of `groups`. The reference program is written for one: setup_inputs(seed, part) draws one part's arguments, and reference() takes and returns one part's arrays. A program takes and returns all parts, laid end to end along the dimension named above; an argument that names none is the same for every part. Nothing has to cross between parts.
Inputs may be any that keep to these rules, and one draw needn't show every extreme that they name: `expert_ids`: the 8 experts of a token differ. In each aligned block of 4 tokens (the tokens of one device), no expert is named by more than 4 tokens, a bound that some block reaches.
All inputs are finite; a program needn't handle non-finite values.
Results may differ from the reference program's by a relative error of at most 0.0064.
Values may be sent and summed in bfloat16 or wider, within the bound.
A program may use at most 128 MiB of HBM per device.

```python
import math
import jax
import jax.numpy as jnp
import numpy as np
from jax import lax

D = 3584
H = 1024
TOP = 8
TOK_DEV = 4
EXPERTS = 16
TOKENS = 64
CAP = 4
N_EXPERT = 16
N_DP = 1


def steps_of(rng, shape, pieces, low, high):
    def one(dim, shards_of):
        draws = jax.random.uniform(jax.random.fold_in(jax.random.fold_in(rng, 6), dim), (shards_of,), jnp.float32, low / len(pieces), high / len(pieces))
        return jnp.repeat(jnp.exp(draws), shape[dim] // shards_of).reshape((-1,) + (1,) * (len(shape) - dim - 1))

    gain = one(*pieces[0])
    for cut in pieces[1:]:
        gain = gain * one(*cut)
    return gain


def routed_block(key, own, number, rows, amount, top, bound, slope):
    order = jax.random.permutation(key, amount)
    crowded, ordinary = portions_of(amount, rows * top, bound, slope, True), portions_of(amount, rows * top, bound, slope, False)
    places = jnp.arange(amount)

    def named(tallies, offset_by):
        used = int((tallies > 0).sum())
        fixed = max(1, used // 4)
        shifted = fixed + (places - fixed + offset_by * (used - fixed)) % max(1, amount - fixed)
        return jnp.zeros((amount,), jnp.int32).at[order[jnp.where(places < fixed, places, shifted)]].set(jnp.asarray(tallies, jnp.int32))

    tallies = jnp.where(number % 4 == 0, named(crowded, number // 4), named(ordinary, number - number // 4 - 1))
    mixed = jax.random.permutation(jax.random.fold_in(own, 3), amount)
    donor, receiver = mixed[0:amount // 2 * 2:2], mixed[1:amount // 2 * 2:2]
    margin = jnp.minimum(tallies[donor] - 1, bound - tallies[receiver]) // 2
    margin = jnp.where((donor == order[0]) | (receiver == order[0]) | (tallies[receiver] == 0), 0, jnp.maximum(margin, 0))
    shifted = jax.random.randint(jax.random.fold_in(own, 4), (amount // 2,), 0, 1 << 20) % (margin + 1)
    tallies = tallies.at[donor].add(-shifted).at[receiver].add(shifted)
    labels = jnp.searchsorted(jnp.cumsum(tallies), jnp.arange(rows * top), side="right").astype(jnp.int32)
    grid = labels.reshape(top, rows).T
    grid = grid[jax.random.permutation(jax.random.fold_in(own, 1), rows)]
    offset_by = jax.random.randint(jax.random.fold_in(own, 2), (rows, 1), 0, top)
    return jnp.take_along_axis(grid, (jnp.arange(top)[None, :] + offset_by) % top, axis=1)


def portions_of(number_of, total, most, lean, full):
    loads = [(1 << 20) // math.isqrt(rank ** lean) + 1 for rank in range(1, number_of + 1)]
    largest = most if full else min(most, max(-(-total // number_of), total * loads[0] // sum(loads)))
    least = 1 if total - largest >= number_of - 1 else 0
    given, spare = [largest] + [least] * (number_of - 1), total - largest - least * (number_of - 1)
    while spare > 0:
        movable = [i for i in range(1, number_of) if given[i] < largest] or [i for i in range(1, number_of) if given[i] < most]
        whole, left = sum([loads[i] for i in movable]), spare
        for i in movable:
            extra = min(most - given[i], max(1, left * loads[i] // whole), spare)
            given[i] = given[i] + extra
            spare = spare - extra
    return np.array(given)


def bell_draw(stream_key, shape, width, limit, cuts=(), held_as=jnp.bfloat16):
    drawn = jax.random.normal(stream_key, shape, jnp.float32) * width
    if len(cuts) > 0:
        drawn = steps_of(stream_key, shape, cuts, -0.22, 0.18) * drawn
    return jnp.clip(drawn, min=-limit, max=limit).astype(held_as)


def setup_inputs(seed: int = 0, part: int = 0) -> dict:
    arg_keys = jax.random.split(jax.random.key(seed), 7)
    part_splits = jax.random.split(jax.random.fold_in(arg_keys[6], part), 7)
    tokens = bell_draw(part_splits[0], (TOKENS, D), 1.0, 6.0, ((0, 16),))
    cotangent = bell_draw(part_splits[1], (TOKENS, D), 0.5, 6.0, ((0, 16),))
    gate = jnp.clip(jnp.exp(math.log(0.5) - 3.224016 * jax.random.uniform(part_splits[2], (TOKENS, TOP), jnp.float32) ** steps_of(part_splits[2], (TOKENS, TOP), ((0, 16),), -0.2, 0.2)), 0.019897461, 0.5).astype(jnp.bfloat16)
    expert_ids_keys = jax.random.split(jax.random.fold_in(part_splits[3], 1), TOKENS // TOK_DEV)
    expert_ids_turns = jax.random.permutation(jax.random.fold_in(part_splits[3], 3), TOKENS // TOK_DEV)
    expert_ids = jax.vmap(lambda own, number: routed_block(jax.random.fold_in(part_splits[3], 2), own, number, TOK_DEV, EXPERTS, TOP, CAP, 2))(expert_ids_keys, expert_ids_turns).reshape((TOKENS, TOP))
    w_in = bell_draw(arg_keys[4], (EXPERTS, D, H), D ** -0.5, 0.09375, ((0, 16),))
    w_out = bell_draw(arg_keys[5], (EXPERTS, H, D), H ** -0.5, 0.1875, ((0, 16),))
    return {"tokens": tokens, "cotangent": cotangent, "gate": gate, "expert_ids": expert_ids, "w_in": w_in, "w_out": w_out}


def reference(tokens, cotangent, gate, expert_ids, w_in, w_out):
    routed = TOKENS * TOP
    slice_width = H // N_DP
    most_rows = N_EXPERT * N_DP * CAP
    flat_ids = expert_ids.reshape(routed)
    onehot = (flat_ids[:, None] == jnp.arange(EXPERTS, dtype=jnp.int32)[None, :]).astype(jnp.int32)
    ranks = jnp.cumsum(onehot, axis=0, dtype=jnp.int32) - 1
    position = jnp.sum(ranks * onehot, axis=1, dtype=jnp.int32)
    table = jnp.full((EXPERTS, most_rows), routed, dtype=jnp.int32)
    table = table.at[flat_ids, position].set(jnp.arange(routed, dtype=jnp.int32))
    row_token = jnp.where(table < routed, table // TOP, TOKENS).astype(jnp.int32)
    tokens_pad = jnp.concatenate([tokens, jnp.zeros((1, D), jnp.bfloat16)], axis=0)
    cot_pad = jnp.concatenate([cotangent, jnp.zeros((1, D), jnp.bfloat16)], axis=0)
    gate_pad = jnp.concatenate([gate.reshape(routed), jnp.zeros((1,), jnp.bfloat16)], axis=0)

    def per_expert(items):
        row_index, token_index, weight_in, weight_out = items
        x_rows = tokens_pad[token_index]
        dy_rows = cot_pad[token_index]
        g_rows = gate_pad[row_index]
        preact = jnp.dot(x_rows, weight_in, preferred_element_type=jnp.float32)
        logistic = jax.nn.sigmoid(preact)
        hidden = (preact * logistic).astype(jnp.bfloat16)
        part_out = jnp.einsum("mjh,jhd->mjd", hidden.reshape(most_rows, N_DP, slice_width).astype(jnp.float32),
                              weight_out.reshape(N_DP, slice_width, D).astype(jnp.float32),
                              precision=lax.Precision.HIGHEST)
        score_parts = jnp.sum(part_out * dy_rows.astype(jnp.float32)[:, None, :], axis=2).astype(jnp.bfloat16)
        score_parts = lax.optimization_barrier(score_parts)
        scores = jnp.sum(score_parts.astype(jnp.float32), axis=1)
        dy_gated = (g_rows.astype(jnp.float32)[:, None] * dy_rows.astype(jnp.float32)).astype(jnp.bfloat16)
        hidden_grad = jnp.dot(dy_gated, weight_out.T, preferred_element_type=jnp.float32)
        preact_grad = (hidden_grad * logistic * (1.0 + preact * (1.0 - logistic))).astype(jnp.bfloat16)
        wout_grad = jnp.dot(hidden.T, dy_gated, preferred_element_type=jnp.float32).astype(jnp.bfloat16)
        win_grad = jnp.dot(x_rows.T, preact_grad, preferred_element_type=jnp.float32).astype(jnp.bfloat16)
        dx_parts = jnp.einsum("mjh,djh->mjd", preact_grad.reshape(most_rows, N_DP, slice_width).astype(jnp.float32),
                              weight_in.reshape(D, N_DP, slice_width).astype(jnp.float32),
                              precision=lax.Precision.HIGHEST).astype(jnp.bfloat16)
        dx_parts = lax.optimization_barrier(dx_parts)
        dx_rows = jnp.sum(dx_parts.astype(jnp.float32), axis=1)
        return win_grad, wout_grad, dx_rows, scores

    w_in_grad, w_out_grad, dx_rows, scores = lax.map(per_expert, (table, row_token, w_in, w_out))
    flat_table = table.reshape(EXPERTS * most_rows)
    dx_all = jnp.zeros((routed + 1, D), jnp.float32).at[flat_table].add(dx_rows.reshape(EXPERTS * most_rows, D))
    tokens_grad = jnp.sum(dx_all[:routed].reshape(TOKENS, TOP, D), axis=1).astype(jnp.bfloat16)
    score_all = jnp.zeros((routed + 1,), jnp.float32).at[flat_table].add(scores.reshape(EXPERTS * most_rows))
    gate_grad = score_all[:routed].reshape(TOKENS, TOP)
    return tokens_grad, gate_grad, w_in_grad, w_out_grad
```

```python
import functools

import jax
import jax.numpy as jnp
from jax import lax
from jax.experimental import pallas as pl
from jax.experimental.pallas import tpu as pltpu
from jax.sharding import PartitionSpec as P

TOP = 8


def build_places(id_block, experts_all, capacity):
    tok_count = id_block.shape[0]
    routed = tok_count * TOP
    slots = experts_all * capacity
    flat_ids = id_block.reshape(routed)
    onehot = (flat_ids[:, None] == jnp.arange(experts_all, dtype=jnp.int32)[None, :]).astype(
        jnp.int32
    )
    ranks = jnp.cumsum(onehot, axis=0, dtype=jnp.int32) - 1
    position = jnp.sum(ranks * onehot, axis=1, dtype=jnp.int32)
    slot_index = flat_ids * capacity + position
    placing = jnp.arange(slots, dtype=jnp.int32)[:, None] == slot_index[None, :]
    place_rows = placing.astype(jnp.bfloat16)
    place_tokens = jnp.sum(placing.reshape(slots, tok_count, TOP).astype(jnp.int32), axis=2).astype(
        jnp.bfloat16
    )
    return (place_rows, place_tokens)


def shards(tokens, cotangent, gate, expert_ids, w_in, w_out):
    tok_count = tokens.shape[0]
    model_width = tokens.shape[1]
    local_experts = w_in.shape[0]
    expert_count = lax.axis_size("expert")
    data_count = lax.axis_size("dp")
    experts_all = local_experts * expert_count
    capacity = min(tok_count, max(2, 2 * tok_count * TOP // experts_all))
    routed = tok_count * TOP
    group_span = data_count * capacity
    group_ids = lax.all_gather(expert_ids, "dp", axis=0, tiled=True)

    def places_of(id_block):
        return build_places(id_block, experts_all, capacity)

    group_place_rows, group_place_tokens = jax.vmap(places_of)(
        group_ids.reshape(data_count, tok_count, TOP)
    )
    token_blocks = group_place_tokens.reshape(data_count, experts_all, capacity, tok_count)
    row_blocks = group_place_rows.reshape(data_count, experts_all, capacity, routed)
    all_tokens, all_cot, all_gate = (
        lax.all_gather(tokens, "dp", axis=0, tiled=True),
        lax.all_gather(cotangent, "dp", axis=0, tiled=True),
        lax.all_gather(gate, "dp", axis=0, tiled=True),
    )
    x_slots = jnp.einsum(
        "ject,jtd->ejcd",
        token_blocks,
        all_tokens.reshape(data_count, tok_count, model_width),
        preferred_element_type=jnp.float32,
    ).astype(jnp.bfloat16)
    dy_slots = jnp.einsum(
        "ject,jtd->ejcd",
        token_blocks,
        all_cot.reshape(data_count, tok_count, model_width),
        preferred_element_type=jnp.float32,
    ).astype(jnp.bfloat16)
    gate_slots = jnp.einsum(
        "jecr,jr->ejc",
        row_blocks,
        all_gate.reshape(data_count, routed),
        preferred_element_type=jnp.float32,
    ).astype(jnp.bfloat16)
    x_in, dy_in, g_in = (
        lax.all_to_all(x_slots, "expert", split_axis=0, concat_axis=0, tiled=True),
        lax.all_to_all(dy_slots, "expert", split_axis=0, concat_axis=0, tiled=True),
        lax.all_to_all(gate_slots, "expert", split_axis=0, concat_axis=0, tiled=True),
    )
    x_in = x_in.reshape(expert_count, local_experts, group_span, model_width)
    dy_in = dy_in.reshape(expert_count, local_experts, group_span, model_width)
    g_in = g_in.reshape(expert_count, local_experts, group_span)
    preact = jnp.einsum("slmd,ldh->slmh", x_in, w_in, preferred_element_type=jnp.float32)
    logistic = jax.nn.sigmoid(preact)
    hidden = (preact * logistic).astype(jnp.bfloat16)
    part_out = jnp.einsum("slmh,lhd->slmd", hidden, w_out, preferred_element_type=jnp.float32)
    score_part = jnp.sum(part_out * dy_in.astype(jnp.float32), axis=3).astype(jnp.bfloat16)
    dy_gated = (g_in.astype(jnp.float32)[..., None] * dy_in.astype(jnp.float32)).astype(
        jnp.bfloat16
    )
    hidden_grad = jnp.einsum("slmd,lhd->slmh", dy_gated, w_out, preferred_element_type=jnp.float32)
    preact_grad = (hidden_grad * logistic * (1.0 + preact * (1.0 - logistic))).astype(jnp.bfloat16)
    w_out_grad = jnp.einsum(
        "slmh,slmd->lhd", hidden, dy_gated, preferred_element_type=jnp.float32
    ).astype(jnp.bfloat16)
    w_in_grad = jnp.einsum(
        "slmd,slmh->ldh", x_in, preact_grad, preferred_element_type=jnp.float32
    ).astype(jnp.bfloat16)
    dx_part = jnp.einsum(
        "slmh,ldh->slmd", preact_grad, w_in, preferred_element_type=jnp.float32
    ).astype(jnp.bfloat16)
    back_rows, back_scores = (
        lax.all_to_all(dx_part, "expert", split_axis=0, concat_axis=0, tiled=True),
        lax.all_to_all(score_part, "expert", split_axis=0, concat_axis=0, tiled=True),
    )
    back_rows = back_rows.reshape(experts_all, data_count, capacity, model_width)
    back_scores = back_scores.reshape(experts_all, data_count, capacity)
    token_part = jnp.einsum(
        "ject,ejcd->jtd", token_blocks, back_rows, preferred_element_type=jnp.float32
    )
    gate_part = jnp.einsum(
        "jecr,ejc->jr", row_blocks, back_scores, preferred_element_type=jnp.float32
    )
    gate_part = gate_part.reshape(data_count, tok_count, TOP)
    token_total, gate_total = (
        lax.psum_scatter(token_part, "dp", scatter_dimension=0, tiled=True),
        lax.psum_scatter(gate_part, "dp", scatter_dimension=0, tiled=True),
    )
    tokens_grad = token_total.reshape(tok_count, model_width).astype(jnp.bfloat16)
    gate_grad = gate_total.reshape(tok_count, TOP)
    return (tokens_grad, gate_grad, w_in_grad, w_out_grad)


F32 = jnp.float32
BF16 = jnp.bfloat16
MESH = pl.DeviceIdType.MESH
VMEM_BYTES = 60 * 1024 * 1024
LANES = 128


def exchange_kernel(
    tok,
    cot,
    gate,
    ids,
    w_in_hbm,
    w_out_hbm,
    x_out,
    dyg_out,
    hid_out,
    dpre_out,
    sum_out,
    w_in,
    w_out,
    tb,
    cb,
    cmat,
    part,
    r1,
    s1,
    r2,
    acc,
    s2,
    r3,
    stage,
    w_sem,
    gather_send,
    gather_recv,
    r1_send,
    r1_recv,
    r2_send,
    r2_recv,
    r3_send,
    r3_recv,
):
    zs = tb.shape[2]
    quarter = tb.shape[4]
    half = part.shape[5]
    blocks = 4 * zs
    rows = 16 * blocks
    count = 4 * blocks
    hidden_units = w_in.shape[1]
    me = lax.axis_index("expert")
    c = lax.rem(me, 2)
    x = lax.rem(lax.div(me, 2), 2)
    z = lax.div(me, 4)

    def index(z_, x_, c_):
        return (z_ * 2 + x_) * 2 + c_

    sibling = index(z, x, 1 - c)
    across = index(z, 1 - x, c)

    weight_copies = [
        pltpu.make_async_copy(w_in_hbm, w_in, w_sem.at[0]),
        pltpu.make_async_copy(w_out_hbm, w_out, w_sem.at[1]),
    ]
    for copy in weight_copies:
        copy.start()

    barrier = pltpu.get_barrier_semaphore()
    peers = [sibling, across] + [index(lax.rem(z + d, zs), x, c) for d in range(1, zs)]
    for peer in peers:
        pl.semaphore_signal(barrier, inc=1, device_id={"expert": peer}, device_id_type=MESH)

    lane = lax.broadcasted_iota(jnp.int32, (4, LANES), 1)
    gates = jnp.zeros((4, LANES), F32)
    gate_f = gate[...].astype(F32)
    ids_v = ids[...]
    for k in range(TOP):
        gates = gates + jnp.where(lane == ids_v[:, k : k + 1], gate_f[:, k : k + 1], 0.0)
    for q in range(4):
        stage[4 * q : 4 * q + 4, 0:quarter] = tok[:, q * quarter : (q + 1) * quarter].astype(F32)
    tb[c, x, z] = stage[:, 0:quarter].astype(BF16)
    stage[:, quarter:] = jnp.zeros((16, LANES), F32)
    stage[0:4, quarter:] = gates
    for q in range(4):
        stage[4 * q : 4 * q + 4, 0:quarter] = cot[:, q * quarter : (q + 1) * quarter].astype(F32)
    cb[c, x, z] = stage[...].astype(BF16)

    pl.semaphore_wait(barrier, len(peers))

    bufs = (tb, cb)
    sent = []

    def remote(a, block, target, slot):
        return pltpu.make_async_remote_copy(
            src_ref=bufs[a].at[block],
            dst_ref=bufs[a].at[block],
            send_sem=gather_send.at[slot],
            recv_sem=gather_recv.at[(a,) + block],
            device_id={"expert": target},
            device_id_type=MESH,
        )

    def under(conds, action):
        if not conds:
            action()
            return
        cond = conds[0]
        for other in conds[1:]:
            cond = jnp.logical_and(cond, other)
        pl.when(cond)(action)

    def send(a, block, target, conds=()):
        slot = len(sent)
        under(conds, lambda: remote(a, block, target, slot).start())
        sent.append((a, block, target, conds))

    def arrive(a, block, conds=()):
        under(conds, lambda: remote(a, block, sibling, 0).wait_recv())

    has_up, has_down = z + 1 < zs, z >= 1
    up = index(jnp.minimum(z + 1, zs - 1), x, c)
    down = index(jnp.maximum(z - 1, 0), x, c)
    own = (c, x, z)
    send(0, own, across)
    send(1, own, up, (has_up,))
    send(1, own, down, (has_down,))
    send(0, own, up, (has_up,))
    send(0, own, down, (has_down,))
    send(1, own, across)
    send(0, own, sibling)
    send(1, own, sibling)
    beside = (c, 1 - x, z)
    arrive(0, beside)
    send(0, beside, up, (has_up,))
    send(0, beside, down, (has_down,))
    send(0, beside, sibling)
    for s in range(1, zs):
        below, above = jnp.maximum(z - s, 0), jnp.minimum(z + s, zs - 1)
        from_below, from_above = z - s >= 0, z + s < zs
        for a, x_ in ((1, x), (0, x), (0, 1 - x)):
            for zz, there, onward, target in (
                (below, from_below, has_up, up),
                (above, from_above, has_down, down),
            ):
                block = (c, x_, zz)
                arrive(a, block, (there,))
                if s < zs - 1:
                    send(a, block, target, (there, onward))
                if a == 1:
                    send(a, block, across, (there,))
                send(a, block, sibling, (there,))
    for d in range(zs):
        block = (c, 1 - x, lax.rem(z + d, zs))
        arrive(1, block)
        send(1, block, sibling)

    def order(shape, dim):
        r = lax.broadcasted_iota(jnp.int32, shape, dim)
        q = lax.div(r, count)
        b = lax.div(lax.rem(r, count), 4)
        return b * 16 + q * 4 + lax.rem(r, 4)

    shape = (rows, rows)
    to_rows = jnp.where(
        order(shape, 0) == lax.broadcasted_iota(jnp.int32, shape, 1), 1.0, 0.0
    ).astype(BF16)
    to_blocks = jnp.where(
        order(shape, 1) == lax.broadcasted_iota(jnp.int32, shape, 0), 1.0, 0.0
    ).astype(BF16)

    for a in range(2):
        for x_ in range(2):
            for zz in range(zs):
                arrive(a, (1 - c, x_, zz))

    x_rows = jnp.dot(to_rows, tb[...].reshape(rows, quarter), preferred_element_type=F32)
    c_rows = jnp.dot(to_rows, cb[...].reshape(rows, quarter + LANES), preferred_element_type=F32)
    lanes = lax.broadcasted_iota(jnp.int32, (count, LANES), 1)
    g = jnp.sum(jnp.where(lanes == me, c_rows[0:count, quarter:], 0.0), axis=1, keepdims=True)
    for q in range(4):
        columns = slice(q * quarter, (q + 1) * quarter)
        x_out[:, columns] = x_rows[q * count : (q + 1) * count].astype(BF16)
        c_q = c_rows[q * count : (q + 1) * count, 0:quarter]
        cmat[:, columns] = c_q.astype(BF16)
        dyg_out[:, columns] = (g * c_q).astype(BF16)

    for copy in weight_copies:
        copy.wait()

    tile = 256

    def hidden_tile(n, score):
        columns = pl.ds(pl.multiple_of(n * tile, tile), tile)
        pre = jnp.dot(x_out[...], w_in[:, columns], preferred_element_type=F32)
        back = lax.dot_general(
            cmat[...], w_out[columns, :], (((1,), (1,)), ((), ())), preferred_element_type=F32
        )
        logistic = jax.nn.sigmoid(pre)
        hidden = (pre * logistic).astype(BF16)
        hid_out[:, columns] = hidden
        dpre_out[:, columns] = (g * back * logistic * (1.0 + pre * (1.0 - logistic))).astype(BF16)
        return score + jnp.sum(hidden.astype(F32) * back, axis=1, keepdims=True)

    score = lax.fori_loop(0, hidden_units // tile, hidden_tile, jnp.zeros((count, 1), F32))
    score_lanes = jnp.where((lanes == me) & (g > 0.0), score, 0.0).astype(BF16)

    def r1_copy(h, x_):
        return pltpu.make_async_remote_copy(
            src_ref=part.at[h, 1 - c, x_],
            dst_ref=r1.at[h, x_],
            send_sem=r1_send.at[h, x_],
            recv_sem=r1_recv.at[h, x_],
            device_id={"expert": sibling},
            device_id_type=MESH,
        )

    def r2_copy(h):
        return pltpu.make_async_remote_copy(
            src_ref=s1.at[h],
            dst_ref=r2.at[h],
            send_sem=r2_send.at[h],
            recv_sem=r2_recv.at[h],
            device_id={"expert": across},
            device_id_type=MESH,
        )

    def r3_copy(h, d, slot):
        to = lax.rem(z + d, zs)
        return pltpu.make_async_remote_copy(
            src_ref=s2.at[h, to],
            dst_ref=r3.at[h, slot],
            send_sem=r3_send.at[h, to],
            recv_sem=r3_recv.at[h, slot],
            device_id={"expert": index(to, x, c)},
            device_id_type=MESH,
        )

    for h in range(2):
        width = half if h == 0 else quarter - half
        pieces = []
        for q in range(4):
            piece = lax.dot_general(
                dpre_out[...],
                w_in[q * quarter + h * half : q * quarter + h * half + width, :],
                (((1,), (1,)), ((), ())),
                preferred_element_type=F32,
            ).astype(BF16)
            if h == 1:
                extra = score_lanes if q == 0 else jnp.zeros((count, LANES), BF16)
                piece = jnp.concatenate([piece, extra], axis=1)
            pieces.append(piece)
        stacked = jnp.concatenate(pieces, axis=0)
        part[h] = (
            jnp.dot(to_blocks, stacked, preferred_element_type=F32)
            .astype(BF16)
            .reshape(2, 2, zs, 16, half)
        )
        r1_copy(h, 1 - x).start()
        r1_copy(h, x).start()

    for h in range(2):
        r1_copy(h, 1 - x).wait_recv()
        s1[h] = (part[h, c, 1 - x].astype(F32) + r1[h, 1 - x].astype(F32)).astype(BF16)
        r2_copy(h).start()
    for h in range(2):
        r1_copy(h, x).wait_recv()
        r2_copy(h).wait_recv()
        total = part[h, c, x].astype(F32) + r1[h, x].astype(F32) + r2[h].astype(F32)
        acc[h] = total
        s2[h] = total.astype(BF16)
        for d in range(1, zs):
            r3_copy(h, d, z).start()
    for h in range(2):
        final = acc[h, z]
        for d in range(1, zs):
            slot = lax.rem(z + d, zs)
            r3_copy(h, d, slot).wait_recv()
            final = final + r3[h, slot].astype(F32)
        sum_out[:, h * half : (h + 1) * half] = final

    for h in range(2):
        r1_copy(h, 0).wait_send()
        r1_copy(h, 1).wait_send()
        r2_copy(h).wait_send()
        for d in range(1, zs):
            r3_copy(h, d, z).wait_send()
    for slot, (a, block, target, conds) in enumerate(sent):
        under(
            conds,
            functools.partial(
                lambda a, block, target, slot: remote(a, block, target, slot).wait_send(),
                a, block, target, slot,
            ),
        )


def grads_kernel(x, dyg, hidden, dpre, sums, ids, tok_grad, gate_grad, w_in_grad, w_out_grad):
    over_rows = (((0,), (0,)), ((), ()))
    w_in_grad[...] = lax.dot_general(
        x[...], dpre[...], over_rows, preferred_element_type=F32
    ).astype(BF16)[None]
    w_out_grad[...] = lax.dot_general(
        hidden[...], dyg[...], over_rows, preferred_element_type=F32
    ).astype(BF16)[None]

    @pl.when(pl.program_id(0) == 0)
    def _():
        quarter = sums.shape[1] - LANES
        for q in range(4):
            tok_grad[:, q * quarter : (q + 1) * quarter] = sums[
                4 * q : 4 * q + 4, 0:quarter
            ].astype(BF16)
        scores = sums[0:4, quarter:]
        lane = lax.broadcasted_iota(jnp.int32, (4, LANES), 1)
        place = lax.broadcasted_iota(jnp.int32, (4, TOP), 1)
        ids_v = ids[...]
        result = jnp.zeros((4, TOP), F32)
        for k in range(TOP):
            value = jnp.sum(
                jnp.where(lane == ids_v[:, k : k + 1], scores, 0.0), axis=1, keepdims=True
            )
            result = jnp.where(place == k, value, result)
        gate_grad[...] = result


def fused_shards(tokens, cotangent, gate, expert_ids, w_in, w_out):
    tok_count, width = tokens.shape
    units = w_in.shape[2]
    zs = lax.axis_size("expert") // 4
    count = 4 * zs * tok_count
    quarter = width // 4
    half = (quarter + LANES) // 2
    vmem = pl.BlockSpec(memory_space=pltpu.VMEM)
    hbm = pl.BlockSpec(memory_space=pl.ANY)
    sends = 10 + 1 + (zs - 1) * 18 + zs
    dma = pltpu.SemaphoreType.DMA
    weight = width * units
    x, dyg, hidden, dpre, sums = pl.pallas_call(
        exchange_kernel,
        out_shape=(
            jax.ShapeDtypeStruct((count, width), BF16),
            jax.ShapeDtypeStruct((count, width), BF16),
            jax.ShapeDtypeStruct((count, units), BF16),
            jax.ShapeDtypeStruct((count, units), BF16),
            jax.ShapeDtypeStruct((16, quarter + LANES), F32),
        ),
        in_specs=[vmem, vmem, vmem, vmem, hbm, hbm],
        out_specs=[vmem] * 5,
        scratch_shapes=[
            pltpu.VMEM((width, units), BF16),
            pltpu.VMEM((units, width), BF16),
            pltpu.VMEM((2, 2, zs, 16, quarter), BF16),
            pltpu.VMEM((2, 2, zs, 16, quarter + LANES), BF16),
            pltpu.VMEM((count, width), BF16),
            pltpu.VMEM((2, 2, 2, zs, 16, half), BF16),
            pltpu.VMEM((2, 2, zs, 16, half), BF16),
            pltpu.VMEM((2, zs, 16, half), BF16),
            pltpu.VMEM((2, zs, 16, half), BF16),
            pltpu.VMEM((2, zs, 16, half), F32),
            pltpu.VMEM((2, zs, 16, half), BF16),
            pltpu.VMEM((2, zs, 16, half), BF16),
            pltpu.VMEM((16, quarter + LANES), F32),
            dma((2,)),
            dma((sends,)),
            dma((2, 2, 2, zs)),
            dma((2, 2)),
            dma((2, 2)),
            dma((2,)),
            dma((2,)),
            dma((2, zs)),
            dma((2, zs)),
        ],
        compiler_params=pltpu.CompilerParams(
            collective_id=0, has_side_effects=True, vmem_limit_bytes=VMEM_BYTES
        ),
        cost_estimate=pl.CostEstimate(
            flops=6 * count * weight, bytes_accessed=4 * weight, transcendentals=count * units
        ),
    )(tokens, cotangent, gate, expert_ids, w_in[0], w_out[0])

    steps = 7
    wide = width // steps
    return pl.pallas_call(
        grads_kernel,
        grid=(steps,),
        out_shape=(
            jax.ShapeDtypeStruct((tok_count, width), BF16),
            jax.ShapeDtypeStruct((tok_count, TOP), F32),
            jax.ShapeDtypeStruct((1, width, units), BF16),
            jax.ShapeDtypeStruct((1, units, width), BF16),
        ),
        in_specs=[
            pl.BlockSpec((count, wide), lambda i: (0, i)),
            pl.BlockSpec((count, wide), lambda i: (0, i)),
            pl.BlockSpec((count, units), lambda i: (0, 0)),
            pl.BlockSpec((count, units), lambda i: (0, 0)),
            pl.BlockSpec((16, quarter + LANES), lambda i: (0, 0)),
            pl.BlockSpec((tok_count, TOP), lambda i: (0, 0)),
        ],
        out_specs=(
            pl.BlockSpec((tok_count, width), lambda i: (0, 0)),
            pl.BlockSpec((tok_count, TOP), lambda i: (0, 0)),
            pl.BlockSpec((1, wide, units), lambda i: (0, i, 0)),
            pl.BlockSpec((1, units, wide), lambda i: (0, 0, i)),
        ),
        compiler_params=pltpu.CompilerParams(vmem_limit_bytes=VMEM_BYTES),
        cost_estimate=pl.CostEstimate(
            flops=4 * count * weight, bytes_accessed=4 * weight, transcendentals=0
        ),
    )(x, dyg, hidden, dpre, sums, expert_ids)


def solution(mesh):
    fused = mesh.shape["dp"] == 1 and mesh.shape["expert"] == 16
    return jax.shard_map(
        fused_shards if fused else shards,
        mesh=mesh,
        in_specs=(
            P(("groups", "expert", "dp"), None),
            P(("groups", "expert", "dp"), None),
            P(("groups", "expert", "dp"), None),
            P(("groups", "expert", "dp"), None),
            P("expert", None, "dp"),
            P("expert", "dp", None),
        ),
        out_specs=(
            P(("groups", "expert", "dp"), None),
            P(("groups", "expert", "dp"), None),
            P(("groups", "expert"), None, "dp"),
            P(("groups", "expert"), "dp", None),
        ),
        check_vma=False,
    )
```

```python
import functools

import jax
import jax.numpy as jnp
from jax import lax
from jax.experimental import pallas as pl
from jax.experimental.pallas import tpu as pltpu
from jax.sharding import PartitionSpec as P

TOP = 8


def build_places(id_block, experts_all, capacity):
    tok_count = id_block.shape[0]
    routed = tok_count * TOP
    slots = experts_all * capacity
    flat_ids = id_block.reshape(routed)
    onehot = (flat_ids[:, None] == jnp.arange(experts_all, dtype=jnp.int32)[None, :]).astype(
        jnp.int32
    )
    ranks = jnp.cumsum(onehot, axis=0, dtype=jnp.int32) - 1
    position = jnp.sum(ranks * onehot, axis=1, dtype=jnp.int32)
    slot_index = flat_ids * capacity + position
    placing = jnp.arange(slots, dtype=jnp.int32)[:, None] == slot_index[None, :]
    place_rows = placing.astype(jnp.bfloat16)
    place_tokens = jnp.sum(placing.reshape(slots, tok_count, TOP).astype(jnp.int32), axis=2).astype(
        jnp.bfloat16
    )
    return (place_rows, place_tokens)


def shards(tokens, cotangent, gate, expert_ids, w_in, w_out):
    tok_count = tokens.shape[0]
    model_width = tokens.shape[1]
    local_experts = w_in.shape[0]
    expert_count = lax.axis_size("expert")
    data_count = lax.axis_size("dp")
    experts_all = local_experts * expert_count
    capacity = min(tok_count, max(2, 2 * tok_count * TOP // experts_all))
    routed = tok_count * TOP
    group_span = data_count * capacity
    group_ids = lax.all_gather(expert_ids, "dp", axis=0, tiled=True)

    def places_of(id_block):
        return build_places(id_block, experts_all, capacity)

    group_place_rows, group_place_tokens = jax.vmap(places_of)(
        group_ids.reshape(data_count, tok_count, TOP)
    )
    token_blocks = group_place_tokens.reshape(data_count, experts_all, capacity, tok_count)
    row_blocks = group_place_rows.reshape(data_count, experts_all, capacity, routed)
    all_tokens, all_cot, all_gate = (
        lax.all_gather(tokens, "dp", axis=0, tiled=True),
        lax.all_gather(cotangent, "dp", axis=0, tiled=True),
        lax.all_gather(gate, "dp", axis=0, tiled=True),
    )
    x_slots = jnp.einsum(
        "ject,jtd->ejcd",
        token_blocks,
        all_tokens.reshape(data_count, tok_count, model_width),
        preferred_element_type=jnp.float32,
    ).astype(jnp.bfloat16)
    dy_slots = jnp.einsum(
        "ject,jtd->ejcd",
        token_blocks,
        all_cot.reshape(data_count, tok_count, model_width),
        preferred_element_type=jnp.float32,
    ).astype(jnp.bfloat16)
    gate_slots = jnp.einsum(
        "jecr,jr->ejc",
        row_blocks,
        all_gate.reshape(data_count, routed),
        preferred_element_type=jnp.float32,
    ).astype(jnp.bfloat16)
    x_in, dy_in, g_in = (
        lax.all_to_all(x_slots, "expert", split_axis=0, concat_axis=0, tiled=True),
        lax.all_to_all(dy_slots, "expert", split_axis=0, concat_axis=0, tiled=True),
        lax.all_to_all(gate_slots, "expert", split_axis=0, concat_axis=0, tiled=True),
    )
    x_in = x_in.reshape(expert_count, local_experts, group_span, model_width)
    dy_in = dy_in.reshape(expert_count, local_experts, group_span, model_width)
    g_in = g_in.reshape(expert_count, local_experts, group_span)
    preact = jnp.einsum("slmd,ldh->slmh", x_in, w_in, preferred_element_type=jnp.float32)
    logistic = jax.nn.sigmoid(preact)
    hidden = (preact * logistic).astype(jnp.bfloat16)
    part_out = jnp.einsum("slmh,lhd->slmd", hidden, w_out, preferred_element_type=jnp.float32)
    score_part = jnp.sum(part_out * dy_in.astype(jnp.float32), axis=3).astype(jnp.bfloat16)
    dy_gated = (g_in.astype(jnp.float32)[..., None] * dy_in.astype(jnp.float32)).astype(
        jnp.bfloat16
    )
    hidden_grad = jnp.einsum("slmd,lhd->slmh", dy_gated, w_out, preferred_element_type=jnp.float32)
    preact_grad = (hidden_grad * logistic * (1.0 + preact * (1.0 - logistic))).astype(jnp.bfloat16)
    w_out_grad = jnp.einsum(
        "slmh,slmd->lhd", hidden, dy_gated, preferred_element_type=jnp.float32
    ).astype(jnp.bfloat16)
    w_in_grad = jnp.einsum(
        "slmd,slmh->ldh", x_in, preact_grad, preferred_element_type=jnp.float32
    ).astype(jnp.bfloat16)
    dx_part = jnp.einsum(
        "slmh,ldh->slmd", preact_grad, w_in, preferred_element_type=jnp.float32
    ).astype(jnp.bfloat16)
    back_rows, back_scores = (
        lax.all_to_all(dx_part, "expert", split_axis=0, concat_axis=0, tiled=True),
        lax.all_to_all(score_part, "expert", split_axis=0, concat_axis=0, tiled=True),
    )
    back_rows = back_rows.reshape(experts_all, data_count, capacity, model_width)
    back_scores = back_scores.reshape(experts_all, data_count, capacity)
    token_part = jnp.einsum(
        "ject,ejcd->jtd", token_blocks, back_rows, preferred_element_type=jnp.float32
    )
    gate_part = jnp.einsum(
        "jecr,ejc->jr", row_blocks, back_scores, preferred_element_type=jnp.float32
    )
    gate_part = gate_part.reshape(data_count, tok_count, TOP)
    token_total, gate_total = (
        lax.psum_scatter(token_part, "dp", scatter_dimension=0, tiled=True),
        lax.psum_scatter(gate_part, "dp", scatter_dimension=0, tiled=True),
    )
    tokens_grad = token_total.reshape(tok_count, model_width).astype(jnp.bfloat16)
    gate_grad = gate_total.reshape(tok_count, TOP)
    return (tokens_grad, gate_grad, w_in_grad, w_out_grad)


F32 = jnp.float32
BF16 = jnp.bfloat16
MESH = pl.DeviceIdType.MESH
VMEM_BYTES = 58 * 1024 * 1024
CHUNKS = 4
LANES = 128


def exchange_kernel(
    tok,
    cot,
    gate,
    ids,
    w_in_hbm,
    w_out_hbm,
    x_out,
    dyg_out,
    hid_out,
    dpre_out,
    sum_out,
    w_in,
    w_out,
    tb,
    cb,
    cmat,
    part,
    r1,
    s1,
    r2,
    acc,
    s2,
    r3,
    stage,
    to_rows,
    to_blocks,
    pre_s,
    w_sem,
    gather_send,
    gather_recv,
    r1_send,
    r1_recv,
    r2_send,
    r2_recv,
    r3_send,
    r3_recv,
):
    zs = tb.shape[2]
    quarter = tb.shape[4]
    half = part.shape[5]
    blocks = 4 * zs
    rows = 16 * blocks
    count = 4 * blocks
    hidden_units = w_in.shape[1]
    me = lax.axis_index("expert")
    c = lax.rem(me, 2)
    x = lax.rem(lax.div(me, 2), 2)
    z = lax.div(me, 4)

    def index(z_, x_, c_):
        return (z_ * 2 + x_) * 2 + c_

    sibling = index(z, x, 1 - c)
    across = index(z, 1 - x, c)

    weight_copies = [
        pltpu.make_async_copy(w_in_hbm, w_in, w_sem.at[0]),
        pltpu.make_async_copy(w_out_hbm, w_out, w_sem.at[1]),
    ]
    for copy in weight_copies:
        copy.start()

    barrier = pltpu.get_barrier_semaphore()
    peers = [sibling, across] + [index(lax.rem(z + d, zs), x, c) for d in range(1, zs)]
    for peer in peers:
        pl.semaphore_signal(barrier, inc=1, device_id={"expert": peer}, device_id_type=MESH)

    lane = lax.broadcasted_iota(jnp.int32, (4, LANES), 1)
    gates = jnp.zeros((4, LANES), F32)
    gate_f = gate[...].astype(F32)
    ids_v = ids[...]
    for k in range(TOP):
        gates = gates + jnp.where(lane == ids_v[:, k : k + 1], gate_f[:, k : k + 1], 0.0)
    for q in range(4):
        stage[4 * q : 4 * q + 4, 0:quarter] = tok[:, q * quarter : (q + 1) * quarter].astype(F32)
    tb[c, x, z] = stage[:, 0:quarter].astype(BF16)
    stage[:, quarter:] = jnp.zeros((16, LANES), F32)
    stage[0:4, quarter:] = gates
    for q in range(4):
        stage[4 * q : 4 * q + 4, 0:quarter] = cot[:, q * quarter : (q + 1) * quarter].astype(F32)
    cb[c, x, z] = stage[...].astype(BF16)

    pl.semaphore_wait(barrier, len(peers))

    bufs = (tb, cb)
    sent = []

    def remote(a, block, target, slot):
        return pltpu.make_async_remote_copy(
            src_ref=bufs[a].at[block],
            dst_ref=bufs[a].at[block],
            send_sem=gather_send.at[slot],
            recv_sem=gather_recv.at[(a,) + block],
            device_id={"expert": target},
            device_id_type=MESH,
        )

    def under(conds, action):
        if not conds:
            action()
            return
        cond = conds[0]
        for other in conds[1:]:
            cond = jnp.logical_and(cond, other)
        pl.when(cond)(action)

    def send(a, block, target, conds=()):
        slot = len(sent)
        under(conds, lambda: remote(a, block, target, slot).start())
        sent.append((a, block, target, conds))

    def arrive(a, block, conds=()):
        under(conds, lambda: remote(a, block, sibling, 0).wait_recv())

    own = (c, x, z)
    for a in range(2):
        for d in range(1, zs):
            zz = lax.rem(z + d, zs)
            send(a, own, index(zz, x, c))
        send(a, own, across)
    send(0, own, sibling)
    send(1, own, sibling)

    low, mid = 4, count.bit_length() - 1

    def order(shape, dim):
        r = lax.broadcasted_iota(jnp.int32, shape, dim)
        q = lax.shift_right_logical(r, mid)
        b = lax.shift_right_logical(r & (count - 1), 2)
        return lax.shift_left(b, low) + lax.shift_left(q, 2) + (r & 3)

    shape = (rows, rows)
    to_rows[...] = jnp.where(
        order(shape, 0) == lax.broadcasted_iota(jnp.int32, shape, 1), 1.0, 0.0
    ).astype(BF16)
    to_blocks[...] = jnp.where(
        order(shape, 1) == lax.broadcasted_iota(jnp.int32, shape, 0), 1.0, 0.0
    ).astype(BF16)

    for a in range(2):
        for d in range(1, zs):
            block = (c, x, lax.rem(z + d, zs))
            arrive(a, block)
            send(a, block, across)
            send(a, block, sibling)
    for d in range(zs):
        block = (c, 1 - x, lax.rem(z + d, zs))
        arrive(0, block)
        send(0, block, sibling)

    for x_ in range(2):
        for zz in range(zs):
            arrive(0, (1 - c, x_, zz))
    x_rows = jnp.dot(to_rows[...], tb[...].reshape(rows, quarter), preferred_element_type=F32)
    for q in range(4):
        x_out[:, q * quarter : (q + 1) * quarter] = x_rows[q * count : (q + 1) * count].astype(BF16)

    weight_copies[0].wait()
    tile = hidden_units // zs
    for n in range(zs):
        columns = slice(n * tile, (n + 1) * tile)
        pre_s[:, columns] = jnp.dot(x_out[...], w_in[:, columns], preferred_element_type=F32)
        block = (c, 1 - x, lax.rem(z + n, zs))
        arrive(1, block)
        send(1, block, sibling)

    for x_ in range(2):
        for zz in range(zs):
            arrive(1, (1 - c, x_, zz))
    c_rows = jnp.dot(to_rows[...], cb[...].reshape(rows, quarter + LANES), preferred_element_type=F32)
    lanes = lax.broadcasted_iota(jnp.int32, (count, LANES), 1)
    g = jnp.sum(jnp.where(lanes == me, c_rows[0:count, quarter:], 0.0), axis=1, keepdims=True)
    for q in range(4):
        columns = slice(q * quarter, (q + 1) * quarter)
        c_q = c_rows[q * count : (q + 1) * count, 0:quarter]
        cmat[:, columns] = c_q.astype(BF16)
        dyg_out[:, columns] = (g * c_q).astype(BF16)

    weight_copies[1].wait()
    score = jnp.zeros((count, 1), F32)
    for n in range(zs):
        columns = slice(n * tile, (n + 1) * tile)
        back = lax.dot_general(
            cmat[...], w_out[columns, :], (((1,), (1,)), ((), ())), preferred_element_type=F32
        )
        pre = pre_s[:, columns]
        logistic = jax.nn.sigmoid(pre)
        hidden = (pre * logistic).astype(BF16)
        hid_out[:, columns] = hidden
        dpre_out[:, columns] = (g * back * logistic * (1.0 + pre * (1.0 - logistic))).astype(BF16)
        score = score + jnp.sum(hidden.astype(F32) * back, axis=1, keepdims=True)
    score_lanes = jnp.where((lanes == me) & (g > 0.0), score, 0.0).astype(BF16)

    def r1_copy(h, x_):
        return pltpu.make_async_remote_copy(
            src_ref=part.at[h, 1 - c, x_],
            dst_ref=r1.at[h, x_],
            send_sem=r1_send.at[h, x_],
            recv_sem=r1_recv.at[h, x_],
            device_id={"expert": sibling},
            device_id_type=MESH,
        )

    def r2_copy(h):
        return pltpu.make_async_remote_copy(
            src_ref=s1.at[h],
            dst_ref=r2.at[h],
            send_sem=r2_send.at[h],
            recv_sem=r2_recv.at[h],
            device_id={"expert": across},
            device_id_type=MESH,
        )

    def r3_copy(h, d, slot):
        to = lax.rem(z + d, zs)
        return pltpu.make_async_remote_copy(
            src_ref=s2.at[h, to],
            dst_ref=r3.at[h, slot],
            send_sem=r3_send.at[h, to],
            recv_sem=r3_recv.at[h, slot],
            device_id={"expert": index(to, x, c)},
            device_id_type=MESH,
        )

    def row_grads(h):
        width = half if h < CHUNKS - 1 else half - LANES
        pieces = []
        for q in range(4):
            piece = lax.dot_general(
                dpre_out[...],
                w_in[q * quarter + h * half : q * quarter + h * half + width, :],
                (((1,), (1,)), ((), ())),
                preferred_element_type=F32,
            ).astype(BF16)
            if width < half:
                extra = score_lanes if q == 0 else jnp.zeros((count, LANES), BF16)
                piece = jnp.concatenate([piece, extra], axis=1)
            pieces.append(piece)
        stacked = jnp.concatenate(pieces, axis=0)
        part[h] = (
            jnp.dot(to_blocks[...], stacked, preferred_element_type=F32)
            .astype(BF16)
            .reshape(2, 2, zs, 16, half)
        )
        r1_copy(h, 1 - x).start()
        r1_copy(h, x).start()

    def add_cores(h):
        r1_copy(h, 1 - x).wait_recv()
        s1[h] = (part[h, c, 1 - x].astype(F32) + r1[h, 1 - x].astype(F32)).astype(BF16)
        r2_copy(h).start()

    def add_across(h):
        r1_copy(h, x).wait_recv()
        r2_copy(h).wait_recv()
        total = part[h, c, x].astype(F32) + r1[h, x].astype(F32) + r2[h].astype(F32)
        acc[h] = total
        s2[h] = total.astype(BF16)
        for d in range(1, zs):
            r3_copy(h, d, z).start()

    row_grads(0)
    row_grads(1)
    add_cores(0)
    row_grads(2)
    add_cores(1)
    row_grads(3)
    add_cores(2)
    add_across(0)
    add_cores(3)
    add_across(1)
    add_across(2)
    add_across(3)
    for h in range(CHUNKS):
        final = acc[h, z]
        for d in range(1, zs):
            slot = lax.rem(z + d, zs)
            r3_copy(h, d, slot).wait_recv()
            final = final + r3[h, slot].astype(F32)
        sum_out[:, h * half : (h + 1) * half] = final

    for h in range(CHUNKS):
        r1_copy(h, 0).wait_send()
        r1_copy(h, 1).wait_send()
        r2_copy(h).wait_send()
        for d in range(1, zs):
            r3_copy(h, d, z).wait_send()
    for slot, (a, block, target, conds) in enumerate(sent):
        under(
            conds,
            functools.partial(
                lambda a, block, target, slot: remote(a, block, target, slot).wait_send(),
                a, block, target, slot,
            ),
        )


def grads_kernel(
    x, dyg, hidden, dpre, sums, ids, tok_grad, gate_grad, w_in_grad, w_out_grad,
    x_t, hidden_t, in_buf, out_buf, in_sem, out_sem,
):
    in_parts, in_rows = in_sem.shape[0], in_buf.shape[0] // in_sem.shape[0]
    out_parts, out_rows = out_sem.shape[0], out_buf.shape[0] // out_sem.shape[0]

    def in_copy(n, rows):
        return pltpu.make_async_copy(in_buf.at[rows], w_in_grad.at[0, rows], in_sem.at[n])

    def out_copy(n, rows):
        return pltpu.make_async_copy(out_buf.at[rows], w_out_grad.at[0, rows], out_sem.at[n])

    for n in range(out_parts):
        rows = pl.ds(n * out_rows, out_rows)
        hidden_t[rows, :] = hidden[:, n * out_rows : (n + 1) * out_rows].T
        out_buf[rows, :] = jnp.dot(
            hidden_t[rows, :], dyg[...], preferred_element_type=F32
        ).astype(BF16)
        out_copy(n, rows).start()
    for n in range(in_parts):
        rows = pl.ds(n * in_rows, in_rows)
        x_t[rows, :] = x[:, n * in_rows : (n + 1) * in_rows].T
        in_buf[rows, :] = jnp.dot(
            x_t[rows, :], dpre[...], preferred_element_type=F32
        ).astype(BF16)
        in_copy(n, rows).start()

    quarter = sums.shape[1] - LANES
    for q in range(4):
        tok_grad[:, q * quarter : (q + 1) * quarter] = sums[4 * q : 4 * q + 4, 0:quarter].astype(BF16)
    scores = sums[0:4, quarter:]
    lane = lax.broadcasted_iota(jnp.int32, (4, LANES), 1)
    place = lax.broadcasted_iota(jnp.int32, (4, TOP), 1)
    ids_v = ids[...]
    result = jnp.zeros((4, TOP), F32)
    for k in range(TOP):
        value = jnp.sum(jnp.where(lane == ids_v[:, k : k + 1], scores, 0.0), axis=1, keepdims=True)
        result = jnp.where(place == k, value, result)
    gate_grad[...] = result

    for n in range(out_parts):
        out_copy(n, pl.ds(n * out_rows, out_rows)).wait()
    for n in range(in_parts):
        in_copy(n, pl.ds(n * in_rows, in_rows)).wait()


def fused_shards(tokens, cotangent, gate, expert_ids, w_in, w_out):
    tok_count, width = tokens.shape
    units = w_in.shape[2]
    zs = lax.axis_size("expert") // 4
    count = 4 * zs * tok_count
    quarter = width // 4
    half = (quarter + LANES) // CHUNKS
    vmem = pl.BlockSpec(memory_space=pltpu.VMEM)
    hbm = pl.BlockSpec(memory_space=pltpu.HBM)
    sends = 10 + 1 + (zs - 1) * 18 + zs
    dma = pltpu.SemaphoreType.DMA
    weight = width * units
    x, dyg, hidden, dpre, sums = pl.pallas_call(
        exchange_kernel,
        out_shape=(
            jax.ShapeDtypeStruct((count, width), BF16),
            jax.ShapeDtypeStruct((count, width), BF16),
            jax.ShapeDtypeStruct((count, units), BF16),
            jax.ShapeDtypeStruct((count, units), BF16),
            jax.ShapeDtypeStruct((16, quarter + LANES), F32),
        ),
        in_specs=[vmem, vmem, vmem, vmem, hbm, hbm],
        out_specs=[vmem] * 5,
        scratch_shapes=[
            pltpu.VMEM((width, units), BF16),
            pltpu.VMEM((units, width), BF16),
            pltpu.VMEM((2, 2, zs, 16, quarter), BF16),
            pltpu.VMEM((2, 2, zs, 16, quarter + LANES), BF16),
            pltpu.VMEM((count, width), BF16),
            pltpu.VMEM((CHUNKS, 2, 2, zs, 16, half), BF16),
            pltpu.VMEM((CHUNKS, 2, zs, 16, half), BF16),
            pltpu.VMEM((CHUNKS, zs, 16, half), BF16),
            pltpu.VMEM((CHUNKS, zs, 16, half), BF16),
            pltpu.VMEM((CHUNKS, zs, 16, half), F32),
            pltpu.VMEM((CHUNKS, zs, 16, half), BF16),
            pltpu.VMEM((CHUNKS, zs, 16, half), BF16),
            pltpu.VMEM((16, quarter + LANES), F32),
            pltpu.VMEM((4 * count, 4 * count), BF16),
            pltpu.VMEM((4 * count, 4 * count), BF16),
            pltpu.VMEM((count, units), F32),
            dma((2,)),
            dma((sends,)),
            dma((2, 2, 2, zs)),
            dma((CHUNKS, 2)),
            dma((CHUNKS, 2)),
            dma((CHUNKS,)),
            dma((CHUNKS,)),
            dma((CHUNKS, zs)),
            dma((CHUNKS, zs)),
        ],
        compiler_params=pltpu.CompilerParams(
            collective_id=0, has_side_effects=True, vmem_limit_bytes=VMEM_BYTES
        ),
        cost_estimate=pl.CostEstimate(
            flops=6 * count * weight, bytes_accessed=4 * weight, transcendentals=count * units
        ),
    )(tokens, cotangent, gate, expert_ids, w_in[0], w_out[0])

    return pl.pallas_call(
        grads_kernel,
        out_shape=(
            jax.ShapeDtypeStruct((tok_count, width), BF16),
            jax.ShapeDtypeStruct((tok_count, TOP), F32),
            jax.ShapeDtypeStruct((1, width, units), BF16),
            jax.ShapeDtypeStruct((1, units, width), BF16),
        ),
        in_specs=[vmem] * 6,
        out_specs=(vmem, vmem, hbm, hbm),
        scratch_shapes=[
            pltpu.VMEM((width, count), BF16),
            pltpu.VMEM((units, count), BF16),
            pltpu.VMEM((width, units), BF16),
            pltpu.VMEM((units, width), BF16),
            dma((14,)),
            dma((8,)),
        ],
        compiler_params=pltpu.CompilerParams(vmem_limit_bytes=VMEM_BYTES),
        cost_estimate=pl.CostEstimate(
            flops=4 * count * weight, bytes_accessed=4 * weight, transcendentals=0
        ),
    )(x, dyg, hidden, dpre, sums, expert_ids)


def solution(mesh):
    fused = mesh.shape["dp"] == 1 and mesh.shape["expert"] == 16
    return jax.shard_map(
        fused_shards if fused else shards,
        mesh=mesh,
        in_specs=(
            P(("groups", "expert", "dp"), None),
            P(("groups", "expert", "dp"), None),
            P(("groups", "expert", "dp"), None),
            P(("groups", "expert", "dp"), None),
            P("expert", None, "dp"),
            P("expert", "dp", None),
        ),
        out_specs=(
            P(("groups", "expert", "dp"), None),
            P(("groups", "expert", "dp"), None),
            P(("groups", "expert"), None, "dp"),
            P(("groups", "expert"), "dp", None),
        ),
        check_vma=False,
    )
```

```python
import functools

import jax
import jax.numpy as jnp
from jax import lax
from jax.experimental import pallas as pl
from jax.experimental.pallas import tpu as pltpu
from jax.sharding import PartitionSpec as P

TOP = 8


def build_places(id_block, experts_all, capacity):
    tok_count = id_block.shape[0]
    routed = tok_count * TOP
    slots = experts_all * capacity
    flat_ids = id_block.reshape(routed)
    onehot = (flat_ids[:, None] == jnp.arange(experts_all, dtype=jnp.int32)[None, :]).astype(
        jnp.int32
    )
    ranks = jnp.cumsum(onehot, axis=0, dtype=jnp.int32) - 1
    position = jnp.sum(ranks * onehot, axis=1, dtype=jnp.int32)
    slot_index = flat_ids * capacity + position
    placing = jnp.arange(slots, dtype=jnp.int32)[:, None] == slot_index[None, :]
    place_rows = placing.astype(jnp.bfloat16)
    place_tokens = jnp.sum(placing.reshape(slots, tok_count, TOP).astype(jnp.int32), axis=2).astype(
        jnp.bfloat16
    )
    return (place_rows, place_tokens)


def shards(tokens, cotangent, gate, expert_ids, w_in, w_out):
    tok_count = tokens.shape[0]
    model_width = tokens.shape[1]
    local_experts = w_in.shape[0]
    expert_count = lax.axis_size("expert")
    data_count = lax.axis_size("dp")
    experts_all = local_experts * expert_count
    capacity = min(tok_count, max(2, 2 * tok_count * TOP // experts_all))
    routed = tok_count * TOP
    group_span = data_count * capacity
    group_ids = lax.all_gather(expert_ids, "dp", axis=0, tiled=True)

    def places_of(id_block):
        return build_places(id_block, experts_all, capacity)

    group_place_rows, group_place_tokens = jax.vmap(places_of)(
        group_ids.reshape(data_count, tok_count, TOP)
    )
    token_blocks = group_place_tokens.reshape(data_count, experts_all, capacity, tok_count)
    row_blocks = group_place_rows.reshape(data_count, experts_all, capacity, routed)
    all_tokens, all_cot, all_gate = (
        lax.all_gather(tokens, "dp", axis=0, tiled=True),
        lax.all_gather(cotangent, "dp", axis=0, tiled=True),
        lax.all_gather(gate, "dp", axis=0, tiled=True),
    )
    x_slots = jnp.einsum(
        "ject,jtd->ejcd",
        token_blocks,
        all_tokens.reshape(data_count, tok_count, model_width),
        preferred_element_type=jnp.float32,
    ).astype(jnp.bfloat16)
    dy_slots = jnp.einsum(
        "ject,jtd->ejcd",
        token_blocks,
        all_cot.reshape(data_count, tok_count, model_width),
        preferred_element_type=jnp.float32,
    ).astype(jnp.bfloat16)
    gate_slots = jnp.einsum(
        "jecr,jr->ejc",
        row_blocks,
        all_gate.reshape(data_count, routed),
        preferred_element_type=jnp.float32,
    ).astype(jnp.bfloat16)
    x_in, dy_in, g_in = (
        lax.all_to_all(x_slots, "expert", split_axis=0, concat_axis=0, tiled=True),
        lax.all_to_all(dy_slots, "expert", split_axis=0, concat_axis=0, tiled=True),
        lax.all_to_all(gate_slots, "expert", split_axis=0, concat_axis=0, tiled=True),
    )
    x_in = x_in.reshape(expert_count, local_experts, group_span, model_width)
    dy_in = dy_in.reshape(expert_count, local_experts, group_span, model_width)
    g_in = g_in.reshape(expert_count, local_experts, group_span)
    preact = jnp.einsum("slmd,ldh->slmh", x_in, w_in, preferred_element_type=jnp.float32)
    logistic = jax.nn.sigmoid(preact)
    hidden = (preact * logistic).astype(jnp.bfloat16)
    part_out = jnp.einsum("slmh,lhd->slmd", hidden, w_out, preferred_element_type=jnp.float32)
    score_part = jnp.sum(part_out * dy_in.astype(jnp.float32), axis=3).astype(jnp.bfloat16)
    dy_gated = (g_in.astype(jnp.float32)[..., None] * dy_in.astype(jnp.float32)).astype(
        jnp.bfloat16
    )
    hidden_grad = jnp.einsum("slmd,lhd->slmh", dy_gated, w_out, preferred_element_type=jnp.float32)
    preact_grad = (hidden_grad * logistic * (1.0 + preact * (1.0 - logistic))).astype(jnp.bfloat16)
    w_out_grad = jnp.einsum(
        "slmh,slmd->lhd", hidden, dy_gated, preferred_element_type=jnp.float32
    ).astype(jnp.bfloat16)
    w_in_grad = jnp.einsum(
        "slmd,slmh->ldh", x_in, preact_grad, preferred_element_type=jnp.float32
    ).astype(jnp.bfloat16)
    dx_part = jnp.einsum(
        "slmh,ldh->slmd", preact_grad, w_in, preferred_element_type=jnp.float32
    ).astype(jnp.bfloat16)
    back_rows, back_scores = (
        lax.all_to_all(dx_part, "expert", split_axis=0, concat_axis=0, tiled=True),
        lax.all_to_all(score_part, "expert", split_axis=0, concat_axis=0, tiled=True),
    )
    back_rows = back_rows.reshape(experts_all, data_count, capacity, model_width)
    back_scores = back_scores.reshape(experts_all, data_count, capacity)
    token_part = jnp.einsum(
        "ject,ejcd->jtd", token_blocks, back_rows, preferred_element_type=jnp.float32
    )
    gate_part = jnp.einsum(
        "jecr,ejc->jr", row_blocks, back_scores, preferred_element_type=jnp.float32
    )
    gate_part = gate_part.reshape(data_count, tok_count, TOP)
    token_total, gate_total = (
        lax.psum_scatter(token_part, "dp", scatter_dimension=0, tiled=True),
        lax.psum_scatter(gate_part, "dp", scatter_dimension=0, tiled=True),
    )
    tokens_grad = token_total.reshape(tok_count, model_width).astype(jnp.bfloat16)
    gate_grad = gate_total.reshape(tok_count, TOP)
    return (tokens_grad, gate_grad, w_in_grad, w_out_grad)


F32 = jnp.float32
BF16 = jnp.bfloat16
MESH = pl.DeviceIdType.MESH
VMEM_BYTES = 58 * 1024 * 1024
CHUNKS = 4
LANES = 128


def exchange_kernel(
    tok,
    cot,
    gate,
    ids,
    w_in_hbm,
    w_out_hbm,
    x_out,
    dyg_out,
    hid_out,
    dpre_out,
    sum_out,
    w_in,
    w_out,
    tb,
    cb,
    cmat,
    part,
    r1,
    s1,
    r2,
    acc,
    s2,
    r3,
    stage,
    to_rows,
    to_blocks,
    pre_s,
    w_sem,
    gather_send,
    gather_recv,
    r1_send,
    r1_recv,
    r2_send,
    r2_recv,
    r3_send,
    r3_recv,
):
    zs = tb.shape[2]
    quarter = tb.shape[4]
    half = part.shape[5]
    blocks = 4 * zs
    rows = 16 * blocks
    count = 4 * blocks
    hidden_units = w_in.shape[1]
    me = lax.axis_index("expert")
    c = lax.rem(me, 2)
    x = lax.rem(lax.div(me, 2), 2)
    z = lax.div(me, 4)

    def index(z_, x_, c_):
        return (z_ * 2 + x_) * 2 + c_

    sibling = index(z, x, 1 - c)
    across = index(z, 1 - x, c)

    weight_copies = [
        pltpu.make_async_copy(w_in_hbm, w_in, w_sem.at[0]),
        pltpu.make_async_copy(w_out_hbm, w_out, w_sem.at[1]),
    ]
    for copy in weight_copies:
        copy.start()

    barrier = pltpu.get_barrier_semaphore()
    peers = [sibling, across] + [index(lax.rem(z + d, zs), x, c) for d in range(1, zs)]
    for peer in peers:
        pl.semaphore_signal(barrier, inc=1, device_id={"expert": peer}, device_id_type=MESH)

    lane = lax.broadcasted_iota(jnp.int32, (4, LANES), 1)
    gates = jnp.zeros((4, LANES), F32)
    gate_f = gate[...].astype(F32)
    ids_v = ids[...]
    for k in range(TOP):
        gates = gates + jnp.where(lane == ids_v[:, k : k + 1], gate_f[:, k : k + 1], 0.0)
    for q in range(4):
        stage[4 * q : 4 * q + 4, 0:quarter] = tok[:, q * quarter : (q + 1) * quarter].astype(F32)
    tb[c, x, z] = stage[:, 0:quarter].astype(BF16)
    stage[:, quarter:] = jnp.zeros((16, LANES), F32)
    stage[0:4, quarter:] = gates
    for q in range(4):
        stage[4 * q : 4 * q + 4, 0:quarter] = cot[:, q * quarter : (q + 1) * quarter].astype(F32)
    cb[c, x, z] = stage[...].astype(BF16)

    pl.semaphore_wait(barrier, len(peers))

    bufs = (tb, cb)
    sent = []

    def remote(a, block, target, slot):
        sem = block if len(block) == 3 else block + (0,)
        return pltpu.make_async_remote_copy(
            src_ref=bufs[a].at[block],
            dst_ref=bufs[a].at[block],
            send_sem=gather_send.at[slot],
            recv_sem=gather_recv.at[(a,) + sem],
            device_id={"expert": target},
            device_id_type=MESH,
        )

    def under(conds, action):
        if not conds:
            action()
            return
        cond = conds[0]
        for other in conds[1:]:
            cond = jnp.logical_and(cond, other)
        pl.when(cond)(action)

    def send(a, block, target, conds=()):
        slot = len(sent)
        under(conds, lambda: remote(a, block, target, slot).start())
        sent.append((a, block, target, conds))

    def arrive(a, block, conds=()):
        under(conds, lambda: remote(a, block, sibling, 0).wait_recv())

    own = (c, x, z)
    for a in range(2):
        for d in (2, 3, 1) if zs == 4 else range(1, zs):
            zz = lax.rem(z + d, zs)
            send(a, own, index(zz, x, c))
        send(a, own, across)

    low, mid = 4, count.bit_length() - 1

    def order(shape, dim):
        r = lax.broadcasted_iota(jnp.int32, shape, dim)
        q = lax.shift_right_logical(r, mid)
        b = lax.shift_right_logical(r & (count - 1), 2)
        return lax.shift_left(b, low) + lax.shift_left(q, 2) + (r & 3)

    shape = (rows, rows)
    to_rows[...] = jnp.where(
        order(shape, 0) == lax.broadcasted_iota(jnp.int32, shape, 1), 1.0, 0.0
    ).astype(BF16)
    to_blocks[...] = jnp.where(
        order(shape, 1) == lax.broadcasted_iota(jnp.int32, shape, 0), 1.0, 0.0
    ).astype(BF16)

    for a in range(2):
        for d in range(1, zs):
            block = (c, x, lax.rem(z + d, zs))
            arrive(a, block)
            send(a, block, across)
        send(a, (c, x), sibling)
    for d in range(zs):
        arrive(0, (c, 1 - x, lax.rem(z + d, zs)))
    send(0, (c, 1 - x), sibling)

    for x_ in range(2):
        arrive(0, (1 - c, x_))
    x_rows = jnp.dot(to_rows[...], tb[...].reshape(rows, quarter), preferred_element_type=F32)
    for q in range(4):
        x_out[:, q * quarter : (q + 1) * quarter] = x_rows[q * count : (q + 1) * count].astype(BF16)

    weight_copies[0].wait()
    tile = hidden_units // zs
    for n in range(zs):
        columns = slice(n * tile, (n + 1) * tile)
        pre_s[:, columns] = jnp.dot(x_out[...], w_in[:, columns], preferred_element_type=F32)
        arrive(1, (c, 1 - x, lax.rem(z + n, zs)))
    send(1, (c, 1 - x), sibling)

    for x_ in range(2):
        arrive(1, (1 - c, x_))
    c_rows = jnp.dot(to_rows[...], cb[...].reshape(rows, quarter + LANES), preferred_element_type=F32)
    lanes = lax.broadcasted_iota(jnp.int32, (count, LANES), 1)
    g = jnp.sum(jnp.where(lanes == me, c_rows[0:count, quarter:], 0.0), axis=1, keepdims=True)
    for q in range(4):
        columns = slice(q * quarter, (q + 1) * quarter)
        c_q = c_rows[q * count : (q + 1) * count, 0:quarter]
        cmat[:, columns] = c_q.astype(BF16)
        dyg_out[:, columns] = (g * c_q).astype(BF16)

    weight_copies[1].wait()
    score = jnp.zeros((count, 1), F32)
    for n in range(zs):
        columns = slice(n * tile, (n + 1) * tile)
        back = lax.dot_general(
            cmat[...], w_out[columns, :], (((1,), (1,)), ((), ())), preferred_element_type=F32
        )
        pre = pre_s[:, columns]
        logistic = jax.nn.sigmoid(pre)
        hidden = (pre * logistic).astype(BF16)
        hid_out[:, columns] = hidden
        dpre_out[:, columns] = (g * back * logistic * (1.0 + pre * (1.0 - logistic))).astype(BF16)
        score = score + jnp.sum(hidden.astype(F32) * back, axis=1, keepdims=True)
    score_lanes = jnp.where((lanes == me) & (g > 0.0), score, 0.0).astype(BF16)

    def r1_copy(h, x_):
        return pltpu.make_async_remote_copy(
            src_ref=part.at[h, 1 - c, x_],
            dst_ref=r1.at[h, x_],
            send_sem=r1_send.at[h, x_],
            recv_sem=r1_recv.at[h, x_],
            device_id={"expert": sibling},
            device_id_type=MESH,
        )

    def r2_copy(h):
        return pltpu.make_async_remote_copy(
            src_ref=s1.at[h],
            dst_ref=r2.at[h],
            send_sem=r2_send.at[h],
            recv_sem=r2_recv.at[h],
            device_id={"expert": across},
            device_id_type=MESH,
        )

    def r3_copy(h, d, slot):
        to = lax.rem(z + d, zs)
        return pltpu.make_async_remote_copy(
            src_ref=s2.at[h, to],
            dst_ref=r3.at[h, slot],
            send_sem=r3_send.at[h, to],
            recv_sem=r3_recv.at[h, slot],
            device_id={"expert": index(to, x, c)},
            device_id_type=MESH,
        )

    def row_grads(h):
        width = half if h < CHUNKS - 1 else half - LANES
        pieces = []
        for q in range(4):
            piece = lax.dot_general(
                dpre_out[...],
                w_in[q * quarter + h * half : q * quarter + h * half + width, :],
                (((1,), (1,)), ((), ())),
                preferred_element_type=F32,
            ).astype(BF16)
            if width < half:
                extra = score_lanes if q == 0 else jnp.zeros((count, LANES), BF16)
                piece = jnp.concatenate([piece, extra], axis=1)
            pieces.append(piece)
        stacked = jnp.concatenate(pieces, axis=0)
        part[h] = (
            jnp.dot(to_blocks[...], stacked, preferred_element_type=F32)
            .astype(BF16)
            .reshape(2, 2, zs, 16, half)
        )
        r1_copy(h, 1 - x).start()
        r1_copy(h, x).start()

    def add_cores(h):
        r1_copy(h, 1 - x).wait_recv()
        s1[h] = (part[h, c, 1 - x].astype(F32) + r1[h, 1 - x].astype(F32)).astype(BF16)
        r2_copy(h).start()

    def add_across(h):
        r1_copy(h, x).wait_recv()
        r2_copy(h).wait_recv()
        total = part[h, c, x].astype(F32) + r1[h, x].astype(F32) + r2[h].astype(F32)
        acc[h] = total
        s2[h] = total.astype(BF16)
        for d in (2, 3, 1) if zs == 4 else range(1, zs):
            r3_copy(h, d, z).start()

    row_grads(0)
    row_grads(1)
    add_cores(0)
    row_grads(2)
    add_cores(1)
    row_grads(3)
    add_cores(2)
    add_across(0)
    add_cores(3)
    add_across(1)
    add_across(2)
    add_across(3)
    for h in range(CHUNKS):
        final = acc[h, z]
        for d in range(1, zs):
            slot = lax.rem(z + d, zs)
            r3_copy(h, d, slot).wait_recv()
            final = final + r3[h, slot].astype(F32)
        sum_out[:, h * half : (h + 1) * half] = final

    for h in range(CHUNKS):
        r1_copy(h, 0).wait_send()
        r1_copy(h, 1).wait_send()
        r2_copy(h).wait_send()
        for d in range(1, zs):
            r3_copy(h, d, z).wait_send()
    for slot, (a, block, target, conds) in enumerate(sent):
        under(
            conds,
            functools.partial(
                lambda a, block, target, slot: remote(a, block, target, slot).wait_send(),
                a, block, target, slot,
            ),
        )


def grads_kernel(
    x, dyg, hidden, dpre, sums, ids, tok_grad, gate_grad, w_in_grad, w_out_grad,
    x_t, hidden_t, in_buf, out_buf, in_sem, out_sem,
):
    in_parts, in_rows = in_sem.shape[0], in_buf.shape[0] // in_sem.shape[0]
    out_parts, out_rows = out_sem.shape[0], out_buf.shape[0] // out_sem.shape[0]

    def in_copy(n, rows):
        return pltpu.make_async_copy(in_buf.at[rows], w_in_grad.at[0, rows], in_sem.at[n])

    def out_copy(n, rows):
        return pltpu.make_async_copy(out_buf.at[rows], w_out_grad.at[0, rows], out_sem.at[n])

    for n in range(out_parts):
        rows = pl.ds(n * out_rows, out_rows)
        hidden_t[rows, :] = hidden[:, n * out_rows : (n + 1) * out_rows].T
        out_buf[rows, :] = jnp.dot(
            hidden_t[rows, :], dyg[...], preferred_element_type=F32
        ).astype(BF16)
        out_copy(n, rows).start()
    for n in range(in_parts):
        rows = pl.ds(n * in_rows, in_rows)
        x_t[rows, :] = x[:, n * in_rows : (n + 1) * in_rows].T
        in_buf[rows, :] = jnp.dot(
            x_t[rows, :], dpre[...], preferred_element_type=F32
        ).astype(BF16)
        in_copy(n, rows).start()

    quarter = sums.shape[1] - LANES
    for q in range(4):
        tok_grad[:, q * quarter : (q + 1) * quarter] = sums[4 * q : 4 * q + 4, 0:quarter].astype(BF16)
    scores = sums[0:4, quarter:]
    lane = lax.broadcasted_iota(jnp.int32, (4, LANES), 1)
    place = lax.broadcasted_iota(jnp.int32, (4, TOP), 1)
    ids_v = ids[...]
    result = jnp.zeros((4, TOP), F32)
    for k in range(TOP):
        value = jnp.sum(jnp.where(lane == ids_v[:, k : k + 1], scores, 0.0), axis=1, keepdims=True)
        result = jnp.where(place == k, value, result)
    gate_grad[...] = result

    for n in range(out_parts):
        out_copy(n, pl.ds(n * out_rows, out_rows)).wait()
    for n in range(in_parts):
        in_copy(n, pl.ds(n * in_rows, in_rows)).wait()


def fused_shards(tokens, cotangent, gate, expert_ids, w_in, w_out):
    tok_count, width = tokens.shape
    units = w_in.shape[2]
    zs = lax.axis_size("expert") // 4
    count = 4 * zs * tok_count
    quarter = width // 4
    half = (quarter + LANES) // CHUNKS
    vmem = pl.BlockSpec(memory_space=pltpu.VMEM)
    hbm = pl.BlockSpec(memory_space=pltpu.HBM)
    sends = 10 + 1 + (zs - 1) * 18 + zs
    dma = pltpu.SemaphoreType.DMA
    weight = width * units
    x, dyg, hidden, dpre, sums = pl.pallas_call(
        exchange_kernel,
        out_shape=(
            jax.ShapeDtypeStruct((count, width), BF16),
            jax.ShapeDtypeStruct((count, width), BF16),
            jax.ShapeDtypeStruct((count, units), BF16),
            jax.ShapeDtypeStruct((count, units), BF16),
            jax.ShapeDtypeStruct((16, quarter + LANES), F32),
        ),
        in_specs=[vmem, vmem, vmem, vmem, hbm, hbm],
        out_specs=[vmem] * 5,
        scratch_shapes=[
            pltpu.VMEM((width, units), BF16),
            pltpu.VMEM((units, width), BF16),
            pltpu.VMEM((2, 2, zs, 16, quarter), BF16),
            pltpu.VMEM((2, 2, zs, 16, quarter + LANES), BF16),
            pltpu.VMEM((count, width), BF16),
            pltpu.VMEM((CHUNKS, 2, 2, zs, 16, half), BF16),
            pltpu.VMEM((CHUNKS, 2, zs, 16, half), BF16),
            pltpu.VMEM((CHUNKS, zs, 16, half), BF16),
            pltpu.VMEM((CHUNKS, zs, 16, half), BF16),
            pltpu.VMEM((CHUNKS, zs, 16, half), F32),
            pltpu.VMEM((CHUNKS, zs, 16, half), BF16),
            pltpu.VMEM((CHUNKS, zs, 16, half), BF16),
            pltpu.VMEM((16, quarter + LANES), F32),
            pltpu.VMEM((4 * count, 4 * count), BF16),
            pltpu.VMEM((4 * count, 4 * count), BF16),
            pltpu.VMEM((count, units), F32),
            dma((2,)),
            dma((sends,)),
            dma((2, 2, 2, zs)),
            dma((CHUNKS, 2)),
            dma((CHUNKS, 2)),
            dma((CHUNKS,)),
            dma((CHUNKS,)),
            dma((CHUNKS, zs)),
            dma((CHUNKS, zs)),
        ],
        compiler_params=pltpu.CompilerParams(
            collective_id=0, has_side_effects=True, vmem_limit_bytes=VMEM_BYTES
        ),
        cost_estimate=pl.CostEstimate(
            flops=6 * count * weight, bytes_accessed=4 * weight, transcendentals=count * units
        ),
    )(tokens, cotangent, gate, expert_ids, w_in[0], w_out[0])

    return pl.pallas_call(
        grads_kernel,
        out_shape=(
            jax.ShapeDtypeStruct((tok_count, width), BF16),
            jax.ShapeDtypeStruct((tok_count, TOP), F32),
            jax.ShapeDtypeStruct((1, width, units), BF16),
            jax.ShapeDtypeStruct((1, units, width), BF16),
        ),
        in_specs=[vmem] * 6,
        out_specs=(vmem, vmem, hbm, hbm),
        scratch_shapes=[
            pltpu.VMEM((width, count), BF16),
            pltpu.VMEM((units, count), BF16),
            pltpu.VMEM((width, units), BF16),
            pltpu.VMEM((units, width), BF16),
            dma((14,)),
            dma((8,)),
        ],
        compiler_params=pltpu.CompilerParams(vmem_limit_bytes=VMEM_BYTES),
        cost_estimate=pl.CostEstimate(
            flops=4 * count * weight, bytes_accessed=4 * weight, transcendentals=0
        ),
    )(x, dyg, hidden, dpre, sums, expert_ids)


def solution(mesh):
    fused = mesh.shape["dp"] == 1 and mesh.shape["expert"] == 16
    return jax.shard_map(
        fused_shards if fused else shards,
        mesh=mesh,
        in_specs=(
            P(("groups", "expert", "dp"), None),
            P(("groups", "expert", "dp"), None),
            P(("groups", "expert", "dp"), None),
            P(("groups", "expert", "dp"), None),
            P("expert", None, "dp"),
            P("expert", "dp", None),
        ),
        out_specs=(
            P(("groups", "expert", "dp"), None),
            P(("groups", "expert", "dp"), None),
            P(("groups", "expert"), None, "dp"),
            P(("groups", "expert"), "dp", None),
        ),
        check_vma=False,
    )
```
